32 devices in a mesh: dp: 2 (over y), gx: 4 (over z), yz: 4 (over x, core).
Axes of the slice: x: 2, y: 2, z: 4, core: 2. Of those that a mesh axis runs over, the one named last changes fastest.
Arguments:
- volume: bfloat16 [2, 4, 16, 4, 2048], P('dp', None, 'gx', 'yz'), may hold values from -6 to 6
- kernel_one: bfloat16 [32, 4, 3, 3, 3], replicated, may hold values from -0.625 to 0.625
- bias_one: float32 [32], replicated, may hold values from -0.5 to 0.5
- kernel_two: bfloat16 [64, 32, 3, 3, 3], replicated, may hold values from -0.625 to 0.625
- bias_two: float32 [64], replicated, may hold values from -0.5 to 0.5
- upstream: bfloat16 [2, 64, 4, 4, 128], P('dp', None, 'gx', 'yz'), may hold values from -6 to 6
Outputs:
- features: bfloat16 [2, 64, 4, 4, 128], P('dp', None, 'gx', 'yz')
- pooled_grad: bfloat16 [2, 32, 8, 4, 512], P('dp', None, 'gx', 'yz')
- kernel_one_grad: float32 [32, 4, 3, 3, 3], replicated
- kernel_two_grad: float32 [64, 32, 3, 3, 3], replicated
The draws below stay inside these ranges and needn't reach their ends.
All inputs are finite; a program needn't handle non-finite values.
Results may differ from the reference program's by a relative error of at most 0.01.
The reference program's roundings to bfloat16 on the way (of `pooled_one`, `second_grad` and `first_grad`) count: a program that leaves them out, or rounds other values in their place, can miss the bound.
Values may be sent and summed in bfloat16 or wider, within the bound.
A program may use at most 64 MiB of HBM per device.

```python
import jax
import jax.numpy as jnp
from jax import lax

CIN = 4
C1 = 32
C2 = 64
ZPARTS = 4
BY = 16
BZ = 128
VOLS = 2
NX = 16
N_YZ = 4


def steps_of(own_key, shape, pieces, least, top_value):
    gain = 1.0
    for position, blocks in pieces:
        steps = jax.random.uniform(jax.random.fold_in(jax.random.fold_in(own_key, 6), position), (blocks,), jnp.float32, least / len(pieces), top_value / len(pieces))
        gain = gain * jnp.repeat(jnp.exp(steps), shape[position] // blocks).reshape((-1,) + (1,) * (len(shape) - 1 - position))
    return gain


def centred(rng, shape, deviation, limit, shards=(), kind=jnp.bfloat16):
    result = deviation * jax.random.normal(rng, shape, jnp.float32)
    if shards:
        result = result * steps_of(rng, shape, shards, -0.22, 0.18)
    return jnp.clip(result, -limit, limit).astype(kind)


def setup_inputs(seed: int = 0) -> dict:
    arg_keys = jax.random.split(jax.random.key(seed), 7)
    return {
        "volume": centred(arg_keys[0], (VOLS, CIN, NX, N_YZ, BY * BZ), 1.0, 6.0, ((0, 2), (2, 4), (3, 4))),
        "kernel_one": centred(arg_keys[1], (C1, CIN, 3, 3, 3), (CIN * 27) ** -0.5, 0.625),
        "bias_one": jnp.clip(jax.random.uniform(arg_keys[2], (C1,), jnp.float32, -0.5, 0.5), -0.5, 0.5),
        "kernel_two": centred(arg_keys[3], (C2, C1, 3, 3, 3), (C1 * 27 // 8) ** -0.5, 0.625),
        "bias_two": jnp.clip(jax.random.uniform(arg_keys[4], (C2,), jnp.float32, -0.5, 0.5), -0.5, 0.5),
        "upstream": centred(arg_keys[5], (VOLS, C2, NX // 4, N_YZ, (BY // 4) * (BZ // 4)), 1.0, 6.0, ((0, 2), (2, 4), (3, 4))),
    }


SLOPE = 0.3

def to_volume(blocks, block_y, block_z):
    extent = blocks.shape
    rows_y = extent[3] // ZPARTS
    shaped = blocks.reshape(extent[0], extent[1], extent[2], rows_y, ZPARTS, block_y, block_z)
    shaped = jnp.transpose(shaped, (0, 1, 2, 3, 5, 4, 6))
    return shaped.reshape(extent[0], extent[1], extent[2], rows_y * block_y, ZPARTS * block_z)

def from_volume(whole, block_y, block_z):
    extent = whole.shape
    rows_y = extent[3] // block_y
    shaped = whole.reshape(extent[0], extent[1], extent[2], rows_y, block_y, ZPARTS, block_z)
    shaped = jnp.transpose(shaped, (0, 1, 2, 3, 5, 4, 6))
    return shaped.reshape(extent[0], extent[1], extent[2], rows_y * ZPARTS, block_y * block_z)

def padded_of(field):
    return jnp.pad(field, ((0, 0), (0, 0), (1, 1), (1, 1), (1, 1)))

def correlate(padded, kernel):
    return lax.conv_general_dilated(padded.astype(jnp.float32), kernel.astype(jnp.float32), (1, 1, 1), 'VALID', dimension_numbers=('NCDHW', 'OIDHW', 'NCDHW'), precision=lax.Precision.HIGHEST)

def kernel_grad(padded, grads):
    summed = lax.conv_general_dilated(padded.astype(jnp.float32), grads.astype(jnp.float32), (1, 1, 1), 'VALID', dimension_numbers=('CNDHW', 'IODHW', 'NCDHW'), precision=lax.Precision.HIGHEST)
    return jnp.transpose(summed, (1, 0, 2, 3, 4))

def average_pool(field):
    extent = field.shape
    shaped = field.reshape(extent[0], extent[1], extent[2] // 2, 2, extent[3] // 2, 2, extent[4] // 2, 2)
    return lax.optimization_barrier(jnp.mean(shaped, axis=(3, 5, 7)))

def spread_back(field):
    extent = field.shape
    wide = jnp.broadcast_to(field[:, :, :, None, :, None, :, None], (extent[0], extent[1], extent[2], 2, extent[3], 2, extent[4], 2))
    return wide.reshape(extent[0], extent[1], extent[2] * 2, extent[3] * 2, extent[4] * 2)

def leaky(values):
    return jnp.where(values > 0, values, SLOPE * values)

def slope_of(values):
    return jnp.where(values > 0, 1.0, SLOPE).astype(values.dtype)

def reference(volume, kernel_one, bias_one, kernel_two, bias_two, upstream):
    whole_in = to_volume(volume, BY, BZ)
    whole_up = to_volume(upstream, BY // 4, BZ // 4)

    def single(pair):
        field = pair[0][None]
        cotangent = pair[1][None]
        padded_in = padded_of(field)
        first_pre = correlate(padded_in, kernel_one) + bias_one[None, :, None, None, None]
        pooled_one = average_pool(leaky(first_pre)).astype(jnp.bfloat16)
        padded_mid = padded_of(pooled_one)
        second_pre = correlate(padded_mid, kernel_two) + bias_two[None, :, None, None, None]
        features = average_pool(leaky(second_pre)).astype(jnp.bfloat16)
        second_grad = (spread_back(cotangent.astype(jnp.float32)) * 0.125 * slope_of(second_pre)).astype(jnp.bfloat16)
        two_grad = kernel_grad(padded_mid, second_grad)
        flipped = jnp.transpose(jnp.flip(kernel_two, (2, 3, 4)), (1, 0, 2, 3, 4))
        pooled_grad = correlate(padded_of(second_grad), flipped).astype(jnp.bfloat16)
        first_grad = (spread_back(pooled_grad.astype(jnp.float32)) * 0.125 * slope_of(first_pre)).astype(jnp.bfloat16)
        one_grad = kernel_grad(padded_in, first_grad)
        return (features[0], pooled_grad[0], one_grad, two_grad)
    features, pooled_grad, one_grads, two_grads = lax.map(single, (whole_in, whole_up))
    return (from_volume(features, BY // 4, BZ // 4), from_volume(pooled_grad, BY // 2, BZ // 2), lax.optimization_barrier(jnp.sum(one_grads, axis=0)) / VOLS, lax.optimization_barrier(jnp.sum(two_grads, axis=0)) / VOLS)
```

```python
import functools

import jax
import jax.numpy as jnp
import numpy as np
from jax import lax
from jax.experimental import pallas as pl
from jax.experimental.pallas import tpu as pltpu
from jax.sharding import PartitionSpec as P

ZPARTS = 4
BY = 16
BZ = 128
SLOPE = 0.3
MESH = pl.DeviceIdType.MESH
F32 = jnp.float32
BF16 = jnp.bfloat16
SIDES = [(dx, dz) for dx in (-1, 0, 1) for dz in (-1, 0, 1) if (dx, dz) != (0, 0)]
PHASES = [(px, pz, py) for px in (0, 1) for pz in (0, 1) for py in (0, 1)]
TAPS = [(kx, ky, kz) for kx in range(3) for ky in range(3) for kz in range(3)]


def split_matrix():
    out = np.zeros((512, 512), np.float32)
    for fy in range(4):
        for fz in range(32):
            for rz in range(4):
                out[fy * 128 + 4 * fz + rz, rz * 128 + fy * 32 + fz] = 1
    return out


def join_matrix():
    out = np.zeros((512, 512), np.float32)
    for pz in range(2):
        for py in range(2):
            for fy in range(4):
                for fz in range(32):
                    out[pz * 256 + py * 128 + fy * 32 + fz, (2 * fy + py) * 64 + 2 * fz + pz] = 1
    return out


def tap_matrix():
    out = np.zeros((128, 8 * 256), np.float32)
    for p, (px, pz, py) in enumerate(PHASES):
        for t, (kx, ky, kz) in enumerate(TAPS):
            for c in range(4):
                row = (px + kx) * 64 + (pz + kz) * 16 + (py + ky) * 4 + c
                out[c * 27 + t, p * 256 + row] = 1
    return out


def dot(a, b):
    return jnp.dot(a, b, preferred_element_type=F32)


def dot_nt(a, b):
    return lax.dot_general(a, b, (((1,), (1,)), ((), ())), preferred_element_type=F32)


def leaky(values):
    return jnp.where(values > 0, values, SLOPE * values)


def slope_of(values):
    return jnp.where(values > 0, 1.0, SLOPE)


def kernel(
    sizes, x_ref, up_ref, k1_ref, b1_ref, k2f_ref, b2_ref, k2b_ref, split_ref, join_ref, taps_ref,
    feat_ref, pg_ref, one_ref, two_ref,
    vol, vol_x, vol_z, vol_d, mid, mid_x, mid_z, mid_d, grad, grad_x, grad_z, grad_d,
    w1, patch, pre1, im_mid, im_grad, flat_grad, part, rs, across, gathered, one_all, one_gx,
    halo_send, halo_recv, plane_send, plane_recv, gx_send, gx_recv,
):
    n_dp, n_gx, n_yz = sizes
    dp, gx, yz = (lax.axis_index("dp"), lax.axis_index("gx"), lax.axis_index("yz"))
    plane = n_dp * n_yz
    rank = dp * n_yz + yz

    def plane_peer(k):
        other = lax.rem(rank + k, plane)
        return other, (other // n_yz, gx, lax.rem(other, n_yz))

    def gx_peer(k):
        other = lax.rem(gx + k, n_gx)
        return other, (dp, other, yz)

    def exists(dx, dz):
        inside = [gx + dx >= 0, gx + dx < n_gx, yz + dz >= 0, yz + dz < n_yz]
        return functools.reduce(jnp.logical_and, inside)

    for ref in (vol_x, vol_z, vol_d, mid_x, mid_z, mid_d, grad_x, grad_z, grad_d):
        ref[...] = jnp.zeros_like(ref)

    barrier = pltpu.get_barrier_semaphore()
    for k in range(1, plane):
        pl.semaphore_signal(barrier, inc=1, device_id=plane_peer(k)[1], device_id_type=MESH)
    for k in range(1, n_gx):
        pl.semaphore_signal(barrier, inc=1, device_id=gx_peer(k)[1], device_id_type=MESH)
    corners = jnp.int32(0)
    for dx, dz in SIDES:
        if dx and dz:
            corners = corners + exists(dx, dz).astype(jnp.int32)

            @pl.when(exists(dx, dz))
            def _(dx=dx, dz=dz):
                pl.semaphore_signal(
                    barrier, inc=1, device_id=(dp, gx + dx, yz + dz), device_id_type=MESH
                )

    def piece(own, dx, dz):
        n = own.shape[0]
        i, j = (n - 1 if dx > 0 else 0, n - 1 if dz > 0 else 0)
        if dx and dz:
            return own.at[i, j]
        return own.at[i] if dx else own.at[:, j]

    def slot(bufs, dx, dz):
        i, j = (int(dx > 0), int(dz > 0))
        if dx and dz:
            return bufs[2].at[i, j]
        return bufs[0].at[i] if dx else bufs[1].at[j]

    def halo_copy(turn, own, bufs, dx, dz):
        return pltpu.make_async_remote_copy(
            src_ref=piece(own, dx, dz),
            dst_ref=slot(bufs, -dx, -dz),
            send_sem=halo_send.at[turn, SIDES.index((dx, dz))],
            recv_sem=halo_recv.at[turn, SIDES.index((-dx, -dz))],
            device_id=(dp, gx + dx, yz + dz),
            device_id_type=MESH,
        )

    def halo_start(turn, own, bufs):
        for dx, dz in SIDES:

            @pl.when(exists(dx, dz))
            def _(dx=dx, dz=dz):
                halo_copy(turn, own, bufs, dx, dz).start()

    def halo_wait(turn, own, bufs):
        for dx, dz in SIDES:

            @pl.when(exists(dx, dz))
            def _(dx=dx, dz=dz):
                halo_copy(turn, own, bufs, dx, dz).wait_send()
                halo_copy(turn, own, bufs, -dx, -dz).wait_recv()

    lanes = lax.broadcasted_iota(jnp.int32, (1, 128), 1)
    cell_z = lanes % 32

    def raw(own, bufs, x, z, more):
        n = own.shape[0]
        dx = -1 if x < 0 else int(x >= n)
        dz = -1 if z < 0 else int(z >= n)
        if not dx and not dz:
            tile = own[(x, z) + more]
        elif dx and dz:
            tile = bufs[2][(int(dx > 0), int(dz > 0)) + more]
        elif dx:
            tile = bufs[0][(int(dx > 0), z) + more]
        else:
            tile = bufs[1][(int(dz > 0), x) + more]
        return tile.astype(F32)

    def roll(tile, by):
        return pltpu.roll(tile, by % 128, 1)

    def along_z(own, bufs, x, z, more=()):
        n = own.shape[0]
        if z < 0:
            inner = roll(raw(own, bufs, x, n - 1, more), 1)
            return jnp.where(cell_z == 0, roll(raw(own, bufs, x, -1, more), -31), inner)
        if z >= n:
            inner = roll(raw(own, bufs, x, 0, more), -1)
            return jnp.where(cell_z == 31, roll(raw(own, bufs, x, n, more), 31), inner)
        return raw(own, bufs, x, z, more)

    def y_before(tile):
        return jnp.where(lanes < 32, 0.0, roll(tile, 32))

    def y_after(tile):
        return jnp.where(lanes >= 96, 0.0, roll(tile, -32))

    def fill(target, own, bufs, flip):
        rows = own.shape[3]
        for ax in range(4):
            for az in range(4):
                tiles = [along_z(own, bufs, ax - 1, az - 1, (y,)) for y in (0, 1)]
                spread = (y_before(tiles[1]), tiles[0], tiles[1], y_after(tiles[0]))
                for ay in range(4):
                    tile = spread[ay].astype(BF16)
                    for p, (px, pz, py) in enumerate(PHASES):
                        tap = (ax - px, ay - py, az - pz)
                        if tap in TAPS:
                            t = TAPS.index(tap)
                            t = 26 - t if flip else t
                            target[t * rows : (t + 1) * rows, p * 128 : (p + 1) * 128] = tile

    by_phase = dot(x_ref[...], split_ref[...])
    for x in range(4):
        for rz in range(4):
            vol[x, rz] = by_phase[x * 16 : x * 16 + 16, rz * 128 : rz * 128 + 128].astype(BF16)
    pl.semaphore_wait(barrier, plane + n_gx - 2 + corners)
    vol_bufs = (vol_x, vol_z, vol_d)
    halo_start(0, vol, vol_bufs)
    for p in range(8):
        chosen = dot(k1_ref[...], taps_ref[:, p * 256 : (p + 1) * 256])
        w1[p * 32 : (p + 1) * 32, :] = chosen.astype(BF16)
    halo_wait(0, vol, vol_bufs)

    rows16 = lax.broadcasted_iota(jnp.int32, (16, 1), 0)
    for ex in range(-1, 5):
        for ez in range(-1, 5):
            tile = along_z(vol, vol_bufs, ex, ez)
            low = pltpu.roll(tile, 4, 0)
            low = jnp.where(rows16 < 4, y_before(low), low).astype(BF16)
            high = pltpu.roll(tile, 12, 0)
            high = jnp.where(rows16 >= 12, y_after(high), high).astype(BF16)
            for q, (qx, qz, qy) in enumerate(PHASES):
                ax, az = (ex + 1 - 2 * qx, ez + 1 - 2 * qz)
                if 0 <= ax < 4 and 0 <= az < 4:
                    row = ax * 64 + az * 16
                    patch[row : row + 16, q * 128 : (q + 1) * 128] = high if qy else low
    for q, (qx, qz, qy) in enumerate(PHASES):
        pre = dot(w1[...], patch[:, q * 128 : (q + 1) * 128])
        total = jnp.zeros((32, 128), F32)
        for p in range(8):
            value = pre[p * 32 : (p + 1) * 32] + b1_ref[...]
            pre1[p * 32 : (p + 1) * 32, q * 128 : (q + 1) * 128] = value
            total = total + leaky(value)
        mid[qx, qz, qy] = (total * 0.125).astype(BF16)

    mid_bufs = (mid_x, mid_z, mid_d)
    halo_start(1, mid, mid_bufs)
    halo_wait(1, mid, mid_bufs)
    fill(im_mid, mid, mid_bufs, False)
    pre2 = dot(k2f_ref[...], im_mid[...])
    total = jnp.zeros((64, 128), F32)
    up = up_ref[...].astype(F32) * 0.125
    for p, (px, pz, py) in enumerate(PHASES):
        value = pre2[:, p * 128 : (p + 1) * 128] + b2_ref[...]
        total = total + leaky(value)
        back = (up * slope_of(value)).astype(BF16)
        grad[px, pz, py] = back
        flat_grad[:, p * 128 : (p + 1) * 128] = back
    grad_bufs = (grad_x, grad_z, grad_d)
    halo_start(2, grad, grad_bufs)
    feat_ref[...] = (total * 0.125).astype(BF16)

    two = dot_nt(flat_grad[...], im_mid[...])
    part_rows = 64 // plane
    part[:, :, 768:896] = jnp.zeros((plane, part_rows, 128), F32)
    part[:, :, 0:864] = two.reshape(plane, part_rows, 864)

    def rs_copy(k):
        other, device = plane_peer(k)
        return pltpu.make_async_remote_copy(
            src_ref=part.at[other], dst_ref=rs.at[k - 1],
            send_sem=plane_send.at[0, k - 1], recv_sem=plane_recv.at[0, k - 1],
            device_id=device, device_id_type=MESH,
        )

    def gx_copy(turn, buf, k):
        other, device = gx_peer(k)
        return pltpu.make_async_remote_copy(
            src_ref=buf.at[gx], dst_ref=buf.at[gx],
            send_sem=gx_send.at[turn, k - 1], recv_sem=gx_recv.at[turn, k - 1],
            device_id=device, device_id_type=MESH,
        )

    def plane_copy(turn, buf, k):
        other, device = plane_peer(k)
        return pltpu.make_async_remote_copy(
            src_ref=buf.at[rank], dst_ref=buf.at[rank],
            send_sem=plane_send.at[turn, k - 1], recv_sem=plane_recv.at[turn, k - 1],
            device_id=device, device_id_type=MESH,
        )

    for k in range(1, plane):
        rs_copy(k).start()

    halo_wait(2, grad, grad_bufs)
    fill(im_grad, grad, grad_bufs, True)
    back1 = dot(k2b_ref[...], im_grad[...]).astype(BF16)
    for px in range(2):
        joined = dot(back1[:, px * 512 : (px + 1) * 512], join_ref[...])
        pg_ref[:, px * 512 : (px + 1) * 512] = joined.astype(BF16)

    for k in range(1, plane):
        rs_copy(k).wait()
    mine = part[rank]
    for k in range(1, plane):
        mine = mine + rs[k - 1]
    across[gx] = mine
    for k in range(1, n_gx):
        gx_copy(0, across, k).start()

    back1 = back1.astype(F32) * 0.125
    folded = jnp.zeros((32, 128), F32)
    for p in range(8):
        grad1 = (back1 * slope_of(pre1[p * 32 : (p + 1) * 32, :])).astype(BF16)
        full = dot_nt(grad1, patch[...])
        high = full.astype(BF16)
        low = (full - high.astype(F32)).astype(BF16)
        choose = taps_ref[:, p * 256 : (p + 1) * 256]
        folded = folded + (dot_nt(high, choose) + dot_nt(low, choose))
    one_all[rank] = folded
    for k in range(1, plane):
        plane_copy(1, one_all, k).start()

    scale = 1.0 / n_dp
    for k in range(1, n_gx):
        gx_copy(0, across, k).wait()
    mine = across[0]
    for j in range(1, n_gx):
        mine = mine + across[j]
    gathered[rank] = mine * scale
    for k in range(1, plane):
        plane_copy(2, gathered, k).start()

    for k in range(1, plane):
        plane_copy(1, one_all, k).wait()
    mine = one_all[0]
    for j in range(1, plane):
        mine = mine + one_all[j]
    one_gx[gx] = mine
    for k in range(1, n_gx):
        gx_copy(1, one_gx, k).start()
    for k in range(1, plane):
        plane_copy(2, gathered, k).wait()
    two_ref[...] = gathered[...]
    for k in range(1, n_gx):
        gx_copy(1, one_gx, k).wait()
    mine = one_gx[0]
    for j in range(1, n_gx):
        mine = mine + one_gx[j]
    one_ref[...] = mine * scale


def local(sizes, volume, kernel_one, bias_one, kernel_two, bias_two, upstream):
    n_dp, n_gx, n_yz = sizes
    plane = n_dp * n_yz
    rows = 64 // plane
    x = volume.reshape(4, 4, 4, 4, 128)
    x = jnp.transpose(x, (1, 3, 0, 2, 4)).reshape(64, 512)
    k1 = jnp.pad(kernel_one.reshape(32, 108), ((0, 0), (0, 20)))
    k2 = kernel_two.reshape(64, 32, 27)
    k2f = jnp.transpose(k2, (0, 2, 1)).reshape(64, 864)
    k2b = jnp.transpose(k2, (1, 2, 0)).reshape(32, 1728)
    vmem = pl.BlockSpec(memory_space=pltpu.VMEM)

    def halos(n, more, rows):
        tile = more + (rows, 128)
        shapes = [(n, n), (2, n), (2, n), (2, 2)]
        return [pltpu.VMEM(s + tile, BF16) for s in shapes]

    feat, pg, one, two = pl.pallas_call(
        functools.partial(kernel, sizes),
        out_shape=(
            jax.ShapeDtypeStruct((64, 128), BF16),
            jax.ShapeDtypeStruct((32, 1024), BF16),
            jax.ShapeDtypeStruct((32, 128), F32),
            jax.ShapeDtypeStruct((plane, rows, 896), F32),
        ),
        in_specs=[vmem] * 10,
        out_specs=(vmem,) * 4,
        scratch_shapes=[
            *halos(4, (), 16),
            *halos(2, (2,), 32),
            *halos(2, (2,), 64),
            pltpu.VMEM((256, 256), BF16),
            pltpu.VMEM((256, 1024), BF16),
            pltpu.VMEM((256, 1024), F32),
            pltpu.VMEM((864, 1024), BF16),
            pltpu.VMEM((1728, 1024), BF16),
            pltpu.VMEM((64, 1024), BF16),
            pltpu.VMEM((plane, rows, 896), F32),
            pltpu.VMEM((plane - 1, rows, 896), F32),
            pltpu.VMEM((n_gx, rows, 896), F32),
            pltpu.VMEM((plane, rows, 896), F32),
            pltpu.VMEM((plane, 32, 128), F32),
            pltpu.VMEM((n_gx, 32, 128), F32),
            pltpu.SemaphoreType.DMA((3, 8)),
            pltpu.SemaphoreType.DMA((3, 8)),
            pltpu.SemaphoreType.DMA((3, plane - 1)),
            pltpu.SemaphoreType.DMA((3, plane - 1)),
            pltpu.SemaphoreType.DMA((2, n_gx - 1)),
            pltpu.SemaphoreType.DMA((2, n_gx - 1)),
        ],
        compiler_params=pltpu.CompilerParams(
            collective_id=0, has_side_effects=True, vmem_limit_bytes=48 * 2**20
        ),
        cost_estimate=pl.CostEstimate(
            flops=900_000_000, bytes_accessed=3_000_000, transcendentals=0
        ),
    )(
        x,
        upstream.reshape(64, 128),
        k1,
        jnp.broadcast_to(bias_one[:, None], (32, 128)),
        k2f,
        jnp.broadcast_to(bias_two[:, None], (64, 128)),
        k2b,
        jnp.asarray(split_matrix(), BF16),
        jnp.asarray(join_matrix(), BF16),
        jnp.asarray(tap_matrix(), BF16),
    )
    two = two.reshape(64, 896)[:, :864].reshape(64, 27, 32)
    two = jnp.transpose(two, (0, 2, 1)).reshape(64, 32, 3, 3, 3)
    return (
        feat.reshape(1, 64, 1, 1, 128),
        pg.reshape(1, 32, 2, 1, 512),
        one[:, :108].reshape(32, 4, 3, 3, 3),
        two,
    )


def wide_with_halo(shard, sides, width):
    for axis, dim in sides:
        size, length = (lax.axis_size(axis), shard.shape[dim])
        up = [(i, (i + 1) % size) for i in range(size - 1)]
        down = [(j, i) for i, j in up]
        last = lax.slice_in_dim(shard, length - width, length, axis=dim)
        leading = lax.slice_in_dim(shard, 0, width, axis=dim)
        before = lax.ppermute(last, axis, up)
        after = lax.ppermute(leading, axis, down)
        shard = jnp.concatenate([before, shard, after], axis=dim)
    return shard


def wide_passed_along(value, axis, steps):
    count = lax.axis_size(axis)
    leading, last = (max(0, -steps), min(count, count - steps))
    return lax.ppermute(value, axis, [(source, source + steps) for source in range(leading, last)])


def wide_correlate(padded, kernel):
    return lax.conv_general_dilated(
        padded,
        kernel,
        (1, 1, 1),
        "VALID",
        dimension_numbers=("NCDHW", "OIDHW", "NCDHW"),
        preferred_element_type=jnp.float32,
    )


def wide_kernel_grad(padded, grads):
    summed = lax.conv_general_dilated(
        padded,
        grads,
        (1, 1, 1),
        "VALID",
        dimension_numbers=("CNDHW", "IODHW", "NCDHW"),
        preferred_element_type=jnp.float32,
    )
    return jnp.transpose(summed, (1, 0, 2, 3, 4))


def wide_average_pool(field):
    extent = field.shape
    shaped = field.reshape(
        extent[0], extent[1], extent[2] // 2, 2, extent[3] // 2, 2, extent[4] // 2, 2
    )
    return jnp.mean(shaped, axis=(3, 5, 7))


def wide_spread_back(field):
    extent = field.shape
    wide = jnp.broadcast_to(
        field[:, :, :, None, :, None, :, None],
        (extent[0], extent[1], extent[2], 2, extent[3], 2, extent[4], 2),
    )
    return wide.reshape(extent[0], extent[1], extent[2] * 2, extent[3] * 2, extent[4] * 2)


def wide_leaky(values):
    return jnp.where(values > 0, values, SLOPE * values)


def wide_slope_of(values):
    return jnp.where(values > 0, 1.0, SLOPE).astype(values.dtype)


def wide_unfold(blocks, block_y, block_z):
    extent = blocks.shape
    return blocks[:, :, :, 0].reshape(extent[0], extent[1], extent[2], block_y, block_z)


def wide_refold(field):
    extent = field.shape
    return field.reshape(extent[0], extent[1], extent[2], 1, extent[3] * extent[4])


def wide_extend(field):
    z_index = lax.axis_index("yz") % ZPARTS
    extended = wide_with_halo(field, (("gx", 2),), 1)
    incoming = []
    for offset, boundary in ((ZPARTS, extended[:, :, :, -1:]), (-ZPARTS, extended[:, :, :, :1])):
        incoming.append(wide_passed_along(boundary, "yz", offset))
    extended = jnp.concatenate([incoming[0], extended, incoming[1]], axis=3)
    arrived = []
    for offset, boundary, keeper in (
        (1, extended[:, :, :, :, -1:], z_index > 0),
        (-1, extended[:, :, :, :, :1], z_index < ZPARTS - 1),
    ):
        moved = wide_passed_along(boundary, "yz", offset)
        arrived.append(jnp.where(keeper, moved, jnp.zeros_like(moved)))
    return jnp.concatenate([arrived[0], extended, arrived[1]], axis=4)


def wide_local(volume, kernel_one, bias_one, kernel_two, bias_two, upstream):
    field = wide_unfold(volume, BY, BZ)
    padded_in = wide_extend(field)
    first_pre = wide_correlate(padded_in, kernel_one) + bias_one[None, :, None, None, None]
    pooled_one = wide_average_pool(wide_leaky(first_pre)).astype(jnp.bfloat16)
    padded_mid = wide_extend(pooled_one)
    second_pre = wide_correlate(padded_mid, kernel_two) + bias_two[None, :, None, None, None]
    features = wide_average_pool(wide_leaky(second_pre)).astype(jnp.bfloat16)
    cotangent = wide_unfold(upstream, BY // 4, BZ // 4).astype(jnp.float32)
    second_grad = (wide_spread_back(cotangent) * 0.125 * wide_slope_of(second_pre)).astype(jnp.bfloat16)
    two_grad = wide_kernel_grad(padded_mid, second_grad)
    replicas = lax.axis_size("dp") * volume.shape[0]
    padded_grad = wide_extend(second_grad)
    flipped = jnp.transpose(jnp.flip(kernel_two, (2, 3, 4)), (1, 0, 2, 3, 4))
    pooled_grad = wide_correlate(padded_grad, flipped).astype(jnp.bfloat16)
    first_grad = (
        wide_spread_back(pooled_grad.astype(jnp.float32)) * 0.125 * wide_slope_of(first_pre)
    ).astype(jnp.bfloat16)
    one_grad = wide_kernel_grad(padded_in, first_grad)
    one_grad, two_grad = lax.psum((one_grad, two_grad), ("dp", "gx", "yz"))
    return (wide_refold(features), wide_refold(pooled_grad), one_grad / replicas, two_grad / replicas)


def solution(mesh):
    sizes = tuple(mesh.shape[name] for name in ("dp", "gx", "yz"))
    one_row = sizes[2] == ZPARTS and 64 % (8 * sizes[0] * sizes[2]) == 0
    return jax.shard_map(
        functools.partial(local, sizes) if one_row else wide_local,
        mesh=mesh,
        in_specs=(
            P("dp", None, "gx", "yz", None),
            P(),
            P(),
            P(),
            P(),
            P("dp", None, "gx", "yz", None),
        ),
        out_specs=(P("dp", None, "gx", "yz", None), P("dp", None, "gx", "yz", None), P(), P()),
        check_vma=False,
    )
```

```python
import functools

import jax
import jax.numpy as jnp
from jax import lax
from jax.experimental import pallas as pl
from jax.experimental.pallas import tpu as pltpu
from jax.sharding import PartitionSpec as P

ZPARTS = 4
BY = 16
BZ = 128
SLOPE = 0.3
MESH = pl.DeviceIdType.MESH
F32 = jnp.float32
BF16 = jnp.bfloat16
SIDES = [(dx, dz) for dx in (-1, 0, 1) for dz in (-1, 0, 1) if (dx, dz) != (0, 0)]
PHASES = [(px, pz, py) for px in (0, 1) for pz in (0, 1) for py in (0, 1)]
TAPS = [(kx, ky, kz) for kx in range(3) for ky in range(3) for kz in range(3)]


def indices(size, dim):
    shape = (1, size) if dim else (size, 1)
    return lax.broadcasted_iota(jnp.int32, shape, dim)


def one_hot(source, rows):
    wide = (rows, source.shape[1])
    row = lax.broadcasted_iota(jnp.int32, wide, 0)
    return jnp.where(row == source, 1.0, 0.0).astype(BF16)


def split_source():
    col = indices(512, 1)
    return (col % 128) // 32 * 128 + 4 * (col % 32) + col // 128


def join_source():
    col = indices(512, 1)
    return col % 2 * 256 + col // 64 % 2 * 128 + col // 128 * 32 + col % 64 // 2


def tap_source(dim):
    at = indices(2048, dim)
    kx = at // 64 % 4 - at // 1024
    kz = at // 16 % 4 - at // 512 % 2
    ky = at // 4 % 4 - at // 256 % 2
    inside = (kx >= 0) & (kx < 3) & (ky >= 0) & (ky < 3) & (kz >= 0) & (kz < 3)
    return jnp.where(inside, ((kx * 3 + ky) * 3 + kz) * 4 + at % 4, -1)


def dot(a, b):
    return jnp.dot(a, b, preferred_element_type=F32)


def dot_nt(a, b):
    return lax.dot_general(a, b, (((1,), (1,)), ((), ())), preferred_element_type=F32)


def leaky(values):
    return jnp.where(values > 0, values, SLOPE * values)


def slope_of(values):
    return jnp.where(values > 0, 1.0, SLOPE)


def kernel(
    sizes, v_ref, up_ref, k1_ref, b1_ref, k2_ref, b2_ref,
    feat_ref, pg_ref, one_ref, two_ref,
    vol, vol_x, vol_z, vol_d, mid, mid_x, mid_z, mid_d, grad, grad_x, grad_z, grad_d,
    w1, patch, pre1, im_mid, im_grad, flat_grad, part, rs, across, gathered, one_all, one_gx,
    cells, k1, k2f, k2b, split, join, taps, taps_t, grads1,
    halo_send, halo_recv, plane_send, plane_recv, gx_send, gx_recv,
):
    n_dp, n_gx, n_yz = sizes
    dp, gx, yz = (lax.axis_index("dp"), lax.axis_index("gx"), lax.axis_index("yz"))
    plane = n_dp * n_yz
    rank = dp * n_yz + yz

    def plane_peer(k):
        other = lax.rem(rank + k, plane)
        return other, (other // n_yz, gx, lax.rem(other, n_yz))

    def gx_peer(k):
        other = lax.rem(gx + k, n_gx)
        return other, (dp, other, yz)

    def exists(dx, dz):
        inside = [gx + dx >= 0, gx + dx < n_gx, yz + dz >= 0, yz + dz < n_yz]
        return functools.reduce(jnp.logical_and, inside)

    barrier = pltpu.get_barrier_semaphore()
    for k in range(1, plane):
        pl.semaphore_signal(barrier, inc=1, device_id=plane_peer(k)[1], device_id_type=MESH)
    for k in range(1, n_gx):
        pl.semaphore_signal(barrier, inc=1, device_id=gx_peer(k)[1], device_id_type=MESH)
    corners = jnp.int32(0)
    for dx, dz in SIDES:
        if dx and dz:
            corners = corners + exists(dx, dz).astype(jnp.int32)

            @pl.when(exists(dx, dz))
            def _(dx=dx, dz=dz):
                pl.semaphore_signal(
                    barrier, inc=1, device_id=(dp, gx + dx, yz + dz), device_id_type=MESH
                )

    def piece(own, dx, dz):
        n = own.shape[0]
        i, j = (n - 1 if dx > 0 else 0, n - 1 if dz > 0 else 0)
        if dx and dz:
            return own.at[i, j]
        return own.at[i] if dx else own.at[:, j]

    def slot(bufs, dx, dz):
        i, j = (int(dx > 0), int(dz > 0))
        if dx and dz:
            return bufs[2].at[i, j]
        return bufs[0].at[i] if dx else bufs[1].at[j]

    sets = ((vol_x, vol_z, vol_d), (mid_x, mid_z, mid_d), (grad_x, grad_z, grad_d))
    for dx, dz in SIDES:

        @pl.when(jnp.logical_not(exists(dx, dz)))
        def _(dx=dx, dz=dz):
            for bufs in sets:
                missing = slot(bufs, dx, dz)
                missing[...] = jnp.zeros_like(missing)

    def halo_copy(turn, own, bufs, dx, dz):
        return pltpu.make_async_remote_copy(
            src_ref=piece(own, dx, dz),
            dst_ref=slot(bufs, -dx, -dz),
            send_sem=halo_send.at[turn, SIDES.index((dx, dz))],
            recv_sem=halo_recv.at[turn, SIDES.index((-dx, -dz))],
            device_id=(dp, gx + dx, yz + dz),
            device_id_type=MESH,
        )

    def halo_start(turn, own, bufs):
        for dx, dz in SIDES:

            @pl.when(exists(dx, dz))
            def _(dx=dx, dz=dz):
                halo_copy(turn, own, bufs, dx, dz).start()

    def halo_wait(turn, own, bufs):
        for dx, dz in SIDES:

            @pl.when(exists(dx, dz))
            def _(dx=dx, dz=dz):
                halo_copy(turn, own, bufs, dx, dz).wait_send()
                halo_copy(turn, own, bufs, -dx, -dz).wait_recv()

    lanes = lax.broadcasted_iota(jnp.int32, (1, 128), 1)
    cell_z = lanes % 32

    def raw(own, bufs, x, z, more):
        n = own.shape[0]
        dx = -1 if x < 0 else int(x >= n)
        dz = -1 if z < 0 else int(z >= n)
        if not dx and not dz:
            tile = own[(x, z) + more]
        elif dx and dz:
            tile = bufs[2][(int(dx > 0), int(dz > 0)) + more]
        elif dx:
            tile = bufs[0][(int(dx > 0), z) + more]
        else:
            tile = bufs[1][(int(dz > 0), x) + more]
        return tile

    def roll(tile, by):
        return pltpu.roll(tile, by % 128, 1)

    def along_z(own, bufs, x, z, more=()):
        n = own.shape[0]
        if 0 <= z < n:
            return raw(own, bufs, x, z, more)
        near = raw(own, bufs, x, n - 1 if z < 0 else 0, more).astype(F32)
        far = raw(own, bufs, x, z, more).astype(F32)
        if z < 0:
            return jnp.where(cell_z == 0, roll(far, -31), roll(near, 1))
        return jnp.where(cell_z == 31, roll(far, 31), roll(near, -1))

    def y_before(tile):
        return jnp.where(lanes < 32, 0.0, roll(tile, 32))

    def y_after(tile):
        return jnp.where(lanes >= 96, 0.0, roll(tile, -32))

    def places(first, end, inner):
        return [
            (x, z)
            for x in range(first, end)
            for z in range(first, end)
            if inner == (first < x < end - 1 and first < z < end - 1)
        ]

    def fill(target, own, bufs, flip, inner):
        rows = own.shape[3]
        for x, z in places(-1, 3, inner):
            ax, az = (x + 1, z + 1)
            tiles = [along_z(own, bufs, x, z, (y,)) for y in (0, 1)]
            after = y_after(tiles[0].astype(F32))
            before = y_before(tiles[1].astype(F32))
            for ay, tile in enumerate((before, tiles[0], tiles[1], after)):
                tile = tile.astype(BF16)
                for p, (px, pz, py) in enumerate(PHASES):
                    tap = (ax - px, ay - py, az - pz)
                    if tap in TAPS:
                        t = TAPS.index(tap)
                        t = 26 - t if flip else t
                        target[t * rows : (t + 1) * rows, p * 128 : (p + 1) * 128] = tile

    rows16 = lax.broadcasted_iota(jnp.int32, (16, 1), 0)

    def fill_patch(inner):
        for ex, ez in places(-1, 5, inner):
            tile = along_z(vol, sets[0], ex, ez).astype(F32)
            low = pltpu.roll(tile, 4, 0)
            low = jnp.where(rows16 < 4, y_before(low), low).astype(BF16)
            high = pltpu.roll(tile, 12, 0)
            high = jnp.where(rows16 >= 12, y_after(high), high).astype(BF16)
            for q, (qx, qz, qy) in enumerate(PHASES):
                ax, az = (ex + 1 - 2 * qx, ez + 1 - 2 * qz)
                if 0 <= ax < 4 and 0 <= az < 4:
                    row = ax * 64 + az * 16
                    patch[row : row + 16, q * 128 : (q + 1) * 128] = high if qy else low

    split[...] = one_hot(split_source(), 512)
    for c in range(4):
        values = v_ref[c].astype(F32)
        for y in range(16):
            fy, ry = (y // 4, y % 4)
            row = ry * 16 + c * 4
            cells[row : row + 4, fy * 128 : (fy + 1) * 128] = values[:, y * 128 : (y + 1) * 128]
    by_phase = dot(cells[...].astype(BF16), split[...]).astype(BF16)
    at = indices(64, 1)
    order = one_hot(at % 4 * 16 + at // 4, 64)
    by_phase = dot(order, by_phase).astype(BF16)
    for x in range(4):
        for rz in range(4):
            vol[x, rz] = by_phase[x * 16 : x * 16 + 16, rz * 128 : rz * 128 + 128]
    pl.semaphore_wait(barrier, plane + n_gx - 2 + corners)
    vol_bufs = sets[0]
    halo_start(0, vol, vol_bufs)

    fill_patch(True)
    k1[...] = jnp.zeros_like(k1)
    for t in range(27):
        k1[t * 4 : t * 4 + 4, 0:32] = k1_ref[t].astype(F32)
    taps[...] = one_hot(tap_source(1), 128)
    flat_k1 = k1[...].T[0:32].astype(BF16)
    for p in range(8):
        chosen = dot(flat_k1, taps[:, p * 256 : (p + 1) * 256])
        w1[p * 32 : (p + 1) * 32, :] = chosen.astype(BF16)
    bias1 = jnp.broadcast_to(b1_ref[...], (128, 32)).T
    bias2 = jnp.broadcast_to(b2_ref[...], (128, 64)).T
    for j in range(7):
        rows = k2_ref[j * 128 : min(j * 128 + 128, 864), :].astype(F32)
        if j == 6:
            rows = jnp.concatenate([rows, jnp.zeros((32, 64), F32)], axis=0)
        k2f[:, j * 128 : (j + 1) * 128] = rows.T.astype(BF16)
    halo_wait(0, vol, vol_bufs)

    fill_patch(False)
    for qx in range(2):
        for qz in range(2):
            q = qx * 4 + qz * 2
            pre = dot(w1[...], patch[:, q * 128 : (q + 2) * 128])
            total = jnp.zeros((32, 256), F32)
            for p in range(8):
                value = pre[p * 32 : (p + 1) * 32] + jnp.concatenate([bias1, bias1], axis=1)
                pre1[p * 32 : (p + 1) * 32, q * 128 : (q + 2) * 128] = value
                total = total + leaky(value)
            for qy in range(2):
                own = total[:, qy * 128 : (qy + 1) * 128]
                mid[qx, qz, qy] = (own * 0.125).astype(BF16)

    mid_bufs = sets[1]
    halo_start(1, mid, mid_bufs)
    fill(im_mid, mid, mid_bufs, False, True)
    for t in range(0, 26, 2):
        pair = [k2_ref[u * 32 : (u + 1) * 32, :].astype(F32) for u in (t, t + 1)]
        k2b[:, t * 64 : (t + 2) * 64] = jnp.concatenate(pair, axis=1).astype(BF16)
    k2b[:, 1664:1728] = k2_ref[832:864, :]
    join[...] = one_hot(join_source(), 512)
    hot = lax.broadcasted_iota(jnp.int32, (2048, 128), 1) == tap_source(0)
    taps_t[...] = jnp.where(hot, 1.0, 0.0).astype(BF16)
    halo_wait(1, mid, mid_bufs)
    fill(im_mid, mid, mid_bufs, False, False)
    pre2 = dot(k2f[:, 0:864], im_mid[...])
    total = jnp.zeros((64, 128), F32)
    up = up_ref[...].astype(F32) * 0.125
    for p, (px, pz, py) in enumerate(PHASES):
        value = pre2[:, p * 128 : (p + 1) * 128] + bias2
        total = total + leaky(value)
        back = (up * slope_of(value)).astype(BF16)
        grad[px, pz, py] = back
        flat_grad[:, p * 128 : (p + 1) * 128] = back
    grad_bufs = sets[2]
    halo_start(2, grad, grad_bufs)
    feat_ref[...] = (total * 0.125).astype(BF16)

    two = dot_nt(flat_grad[...], im_mid[...])
    part_rows = 64 // plane
    part[:, :, 768:896] = jnp.zeros((plane, part_rows, 128), F32)
    part[:, :, 0:864] = two.reshape(plane, part_rows, 864)

    def rs_copy(k):
        other, device = plane_peer(k)
        return pltpu.make_async_remote_copy(
            src_ref=part.at[other], dst_ref=rs.at[k - 1],
            send_sem=plane_send.at[0, k - 1], recv_sem=plane_recv.at[0, k - 1],
            device_id=device, device_id_type=MESH,
        )

    def gx_copy(turn, buf, k):
        other, device = gx_peer(k)
        return pltpu.make_async_remote_copy(
            src_ref=buf.at[gx], dst_ref=buf.at[gx],
            send_sem=gx_send.at[turn, k - 1], recv_sem=gx_recv.at[turn, k - 1],
            device_id=device, device_id_type=MESH,
        )

    def plane_copy(turn, buf, k):
        other, device = plane_peer(k)
        return pltpu.make_async_remote_copy(
            src_ref=buf.at[rank], dst_ref=buf.at[rank],
            send_sem=plane_send.at[turn, k - 1], recv_sem=plane_recv.at[turn, k - 1],
            device_id=device, device_id_type=MESH,
        )

    for k in range(1, plane):
        rs_copy(k).start()

    fill(im_grad, grad, grad_bufs, True, True)
    halo_wait(2, grad, grad_bufs)
    fill(im_grad, grad, grad_bufs, True, False)
    rounded = dot(k2b[...], im_grad[...]).astype(BF16)

    for k in range(1, plane):
        rs_copy(k).wait()
    mine = part[rank]
    for k in range(1, plane):
        mine = mine + rs[k - 1]
    across[gx] = mine
    for k in range(1, n_gx):
        gx_copy(0, across, k).start()

    back1 = rounded.astype(F32) * 0.125
    for p in range(8):
        slope = slope_of(pre1[p * 32 : (p + 1) * 32, :])
        grads1[p * 32 : (p + 1) * 32, :] = (back1 * slope).astype(BF16)
    full = dot_nt(grads1[...], patch[...])
    full = jnp.concatenate([full[p * 32 : (p + 1) * 32] for p in range(8)], axis=1)
    high = full.astype(BF16)
    low = (full - high.astype(F32)).astype(BF16)
    folded = dot(jnp.concatenate([high, low], axis=0), taps_t[...])
    folded = folded[0:32] + folded[32:64]
    one_all[rank] = folded
    for k in range(1, plane):
        plane_copy(1, one_all, k).start()

    for px in range(2):
        joined = dot(rounded[:, px * 512 : (px + 1) * 512], join[...])
        pg_ref[:, px * 512 : (px + 1) * 512] = joined.astype(BF16)

    scale = 1.0 / n_dp
    for k in range(1, n_gx):
        gx_copy(0, across, k).wait()
    mine = across[0]
    for j in range(1, n_gx):
        mine = mine + across[j]
    gathered[rank] = mine * scale
    for k in range(1, plane):
        plane_copy(2, gathered, k).start()

    for k in range(1, plane):
        plane_copy(1, one_all, k).wait()
    mine = one_all[0]
    for j in range(1, plane):
        mine = mine + one_all[j]
    one_gx[gx] = mine
    for k in range(1, n_gx):
        gx_copy(1, one_gx, k).start()
    for k in range(1, plane):
        plane_copy(2, gathered, k).wait()
    whole = gathered[...].reshape(64, 896)
    for j in range(7):
        end = min(j * 128 + 128, 864)
        two_ref[j * 128 : end, :] = whole[:, j * 128 : (j + 1) * 128].T[0 : end - j * 128]
    for k in range(1, n_gx):
        gx_copy(1, one_gx, k).wait()
    mine = one_gx[0]
    for j in range(1, n_gx):
        mine = mine + one_gx[j]
    mine = (mine * scale).T
    for t in range(27):
        one_ref[t] = mine[t * 4 : t * 4 + 4]


def local(sizes, volume, kernel_one, bias_one, kernel_two, bias_two, upstream):
    n_dp, n_gx, n_yz = sizes
    plane = n_dp * n_yz
    rows = 64 // plane
    vmem = pl.BlockSpec(memory_space=pltpu.VMEM)

    def halos(n, more, rows):
        tile = more + (rows, 128)
        shapes = [(n, n), (2, n), (2, n), (2, 2)]
        return [pltpu.VMEM(s + tile, BF16) for s in shapes]

    feat, pg, one, two = pl.pallas_call(
        functools.partial(kernel, sizes),
        out_shape=(
            jax.ShapeDtypeStruct((64, 128), BF16),
            jax.ShapeDtypeStruct((32, 1024), BF16),
            jax.ShapeDtypeStruct((27, 4, 32), F32),
            jax.ShapeDtypeStruct((864, 64), F32),
        ),
        in_specs=[vmem] * 6,
        out_specs=(vmem,) * 4,
        scratch_shapes=[
            *halos(4, (), 16),
            *halos(2, (2,), 32),
            *halos(2, (2,), 64),
            pltpu.VMEM((256, 256), BF16),
            pltpu.VMEM((256, 1024), BF16),
            pltpu.VMEM((256, 1024), F32),
            pltpu.VMEM((864, 1024), BF16),
            pltpu.VMEM((1728, 1024), BF16),
            pltpu.VMEM((64, 1024), BF16),
            pltpu.VMEM((plane, rows, 896), F32),
            pltpu.VMEM((plane - 1, rows, 896), F32),
            pltpu.VMEM((n_gx, rows, 896), F32),
            pltpu.VMEM((plane, rows, 896), F32),
            pltpu.VMEM((plane, 32, 128), F32),
            pltpu.VMEM((n_gx, 32, 128), F32),
            pltpu.VMEM((64, 512), F32),
            pltpu.VMEM((128, 128), F32),
            pltpu.VMEM((64, 896), BF16),
            pltpu.VMEM((32, 1728), BF16),
            pltpu.VMEM((512, 512), BF16),
            pltpu.VMEM((512, 512), BF16),
            pltpu.VMEM((128, 2048), BF16),
            pltpu.VMEM((2048, 128), BF16),
            pltpu.VMEM((256, 1024), BF16),
            pltpu.SemaphoreType.DMA((3, 8)),
            pltpu.SemaphoreType.DMA((3, 8)),
            pltpu.SemaphoreType.DMA((3, plane - 1)),
            pltpu.SemaphoreType.DMA((3, plane - 1)),
            pltpu.SemaphoreType.DMA((2, n_gx - 1)),
            pltpu.SemaphoreType.DMA((2, n_gx - 1)),
        ],
        compiler_params=pltpu.CompilerParams(
            collective_id=0, has_side_effects=True, vmem_limit_bytes=48 * 2**20
        ),
        cost_estimate=pl.CostEstimate(
            flops=900_000_000, bytes_accessed=3_000_000, transcendentals=0
        ),
    )(
        volume.reshape(4, 4, 2048),
        upstream.reshape(64, 128),
        jnp.transpose(kernel_one, (2, 3, 4, 1, 0)).reshape(27, 4, 32),
        bias_one.reshape(1, 32),
        jnp.transpose(kernel_two, (2, 3, 4, 1, 0)).reshape(864, 64),
        bias_two.reshape(1, 64),
    )
    return (
        feat.reshape(1, 64, 1, 1, 128),
        pg.reshape(1, 32, 2, 1, 512),
        jnp.transpose(one.reshape(3, 3, 3, 4, 32), (4, 3, 0, 1, 2)),
        jnp.transpose(two.reshape(3, 3, 3, 32, 64), (4, 3, 0, 1, 2)),
    )


def wide_with_halo(shard, sides, width):
    for axis, dim in sides:
        size, length = (lax.axis_size(axis), shard.shape[dim])
        up = [(i, (i + 1) % size) for i in range(size - 1)]
        down = [(j, i) for i, j in up]
        last = lax.slice_in_dim(shard, length - width, length, axis=dim)
        leading = lax.slice_in_dim(shard, 0, width, axis=dim)
        before = lax.ppermute(last, axis, up)
        after = lax.ppermute(leading, axis, down)
        shard = jnp.concatenate([before, shard, after], axis=dim)
    return shard


def wide_passed_along(value, axis, steps):
    count = lax.axis_size(axis)
    leading, last = (max(0, -steps), min(count, count - steps))
    return lax.ppermute(value, axis, [(source, source + steps) for source in range(leading, last)])


def wide_correlate(padded, kernel):
    return lax.conv_general_dilated(
        padded,
        kernel,
        (1, 1, 1),
        "VALID",
        dimension_numbers=("NCDHW", "OIDHW", "NCDHW"),
        preferred_element_type=jnp.float32,
    )


def wide_kernel_grad(padded, grads):
    summed = lax.conv_general_dilated(
        padded,
        grads,
        (1, 1, 1),
        "VALID",
        dimension_numbers=("CNDHW", "IODHW", "NCDHW"),
        preferred_element_type=jnp.float32,
    )
    return jnp.transpose(summed, (1, 0, 2, 3, 4))


def wide_average_pool(field):
    extent = field.shape
    shaped = field.reshape(
        extent[0], extent[1], extent[2] // 2, 2, extent[3] // 2, 2, extent[4] // 2, 2
    )
    return jnp.mean(shaped, axis=(3, 5, 7))


def wide_spread_back(field):
    extent = field.shape
    wide = jnp.broadcast_to(
        field[:, :, :, None, :, None, :, None],
        (extent[0], extent[1], extent[2], 2, extent[3], 2, extent[4], 2),
    )
    return wide.reshape(extent[0], extent[1], extent[2] * 2, extent[3] * 2, extent[4] * 2)


def wide_leaky(values):
    return jnp.where(values > 0, values, SLOPE * values)


def wide_slope_of(values):
    return jnp.where(values > 0, 1.0, SLOPE).astype(values.dtype)


def wide_unfold(blocks, block_y, block_z):
    extent = blocks.shape
    return blocks[:, :, :, 0].reshape(extent[0], extent[1], extent[2], block_y, block_z)


def wide_refold(field):
    extent = field.shape
    return field.reshape(extent[0], extent[1], extent[2], 1, extent[3] * extent[4])


def wide_extend(field):
    z_index = lax.axis_index("yz") % ZPARTS
    extended = wide_with_halo(field, (("gx", 2),), 1)
    incoming = []
    for offset, boundary in ((ZPARTS, extended[:, :, :, -1:]), (-ZPARTS, extended[:, :, :, :1])):
        incoming.append(wide_passed_along(boundary, "yz", offset))
    extended = jnp.concatenate([incoming[0], extended, incoming[1]], axis=3)
    arrived = []
    for offset, boundary, keeper in (
        (1, extended[:, :, :, :, -1:], z_index > 0),
        (-1, extended[:, :, :, :, :1], z_index < ZPARTS - 1),
    ):
        moved = wide_passed_along(boundary, "yz", offset)
        arrived.append(jnp.where(keeper, moved, jnp.zeros_like(moved)))
    return jnp.concatenate([arrived[0], extended, arrived[1]], axis=4)


def wide_local(volume, kernel_one, bias_one, kernel_two, bias_two, upstream):
    field = wide_unfold(volume, BY, BZ)
    padded_in = wide_extend(field)
    first_pre = wide_correlate(padded_in, kernel_one) + bias_one[None, :, None, None, None]
    pooled_one = wide_average_pool(wide_leaky(first_pre)).astype(jnp.bfloat16)
    padded_mid = wide_extend(pooled_one)
    second_pre = wide_correlate(padded_mid, kernel_two) + bias_two[None, :, None, None, None]
    features = wide_average_pool(wide_leaky(second_pre)).astype(jnp.bfloat16)
    cotangent = wide_unfold(upstream, BY // 4, BZ // 4).astype(jnp.float32)
    second_grad = (wide_spread_back(cotangent) * 0.125 * wide_slope_of(second_pre)).astype(jnp.bfloat16)
    two_grad = wide_kernel_grad(padded_mid, second_grad)
    replicas = lax.axis_size("dp") * volume.shape[0]
    padded_grad = wide_extend(second_grad)
    flipped = jnp.transpose(jnp.flip(kernel_two, (2, 3, 4)), (1, 0, 2, 3, 4))
    pooled_grad = wide_correlate(padded_grad, flipped).astype(jnp.bfloat16)
    first_grad = (
        wide_spread_back(pooled_grad.astype(jnp.float32)) * 0.125 * wide_slope_of(first_pre)
    ).astype(jnp.bfloat16)
    one_grad = wide_kernel_grad(padded_in, first_grad)
    one_grad, two_grad = lax.psum((one_grad, two_grad), ("dp", "gx", "yz"))
    return (wide_refold(features), wide_refold(pooled_grad), one_grad / replicas, two_grad / replicas)


def solution(mesh):
    sizes = tuple(mesh.shape[name] for name in ("dp", "gx", "yz"))
    one_row = sizes[2] == ZPARTS and 64 % (8 * sizes[0] * sizes[2]) == 0
    return jax.shard_map(
        functools.partial(local, sizes) if one_row else wide_local,
        mesh=mesh,
        in_specs=(
            P("dp", None, "gx", "yz", None),
            P(),
            P(),
            P(),
            P(),
            P("dp", None, "gx", "yz", None),
        ),
        out_specs=(P("dp", None, "gx", "yz", None), P("dp", None, "gx", "yz", None), P(), P()),
        check_vma=False,
    )
```

```python
import functools

import jax
import jax.numpy as jnp
from jax import lax
from jax.experimental import pallas as pl
from jax.experimental.pallas import tpu as pltpu
from jax.sharding import PartitionSpec as P

ZPARTS = 4
BY = 16
BZ = 128
SLOPE = 0.3
MESH = pl.DeviceIdType.MESH
F32 = jnp.float32
BF16 = jnp.bfloat16
SIDES = [(dx, dz) for dx in (-1, 0, 1) for dz in (-1, 0, 1) if (dx, dz) != (0, 0)]
PHASES = [(px, pz, py) for px in (0, 1) for pz in (0, 1) for py in (0, 1)]
TAPS = [(kx, ky, kz) for kx in range(3) for ky in range(3) for kz in range(3)]


def indices(size, dim):
    shape = (1, size) if dim else (size, 1)
    return lax.broadcasted_iota(jnp.int32, shape, dim)


def one_hot(source, rows):
    wide = (rows, source.shape[1])
    row = lax.broadcasted_iota(jnp.int32, wide, 0)
    return jnp.where(row == source, 1.0, 0.0).astype(BF16)


def split_source():
    col = indices(512, 1)
    return (col % 128) // 32 * 128 + 4 * (col % 32) + col // 128


def join_source():
    col = indices(512, 1)
    return col % 2 * 256 + col // 64 % 2 * 128 + col // 128 * 32 + col % 64 // 2


def tap_source(dim):
    at = indices(2048, dim)
    kx = at // 64 % 4 - at // 1024
    kz = at // 16 % 4 - at // 512 % 2
    ky = at // 4 % 4 - at // 256 % 2
    inside = (kx >= 0) & (kx < 3) & (ky >= 0) & (ky < 3) & (kz >= 0) & (kz < 3)
    return jnp.where(inside, ((kx * 3 + ky) * 3 + kz) * 4 + at % 4, -1)


def dot(a, b):
    return jnp.dot(a, b, preferred_element_type=F32)


def dot_nt(a, b):
    return lax.dot_general(a, b, (((1,), (1,)), ((), ())), preferred_element_type=F32)


def leaky(values):
    return jnp.where(values > 0, values, SLOPE * values)


def slope_of(values):
    return jnp.where(values > 0, 1.0, SLOPE)


def kernel(
    sizes, v_hbm, up_hbm, k1_hbm, b1_hbm, k2_hbm, b2_hbm,
    feat_ref, pg_ref, one_ref, two_ref,
    vol, vol_x, vol_z, vol_d, mid, mid_x, mid_z, mid_d, grad, grad_x, grad_z, grad_d,
    w1, patch, pre1, im_mid, im_grad, flat_grad, part, rs, across, gathered, one_all, one_gx,
    cells, k1, k2f, k2b, split, join, taps, taps_t, grads1,
    v_ref, up_ref, k1_ref, b1_ref, k2_ref, b2_ref, load_sem,
    halo_send, halo_recv, plane_send, plane_recv, gx_send, gx_recv,
):
    n_dp, n_gx, n_yz = sizes
    dp, gx, yz = (lax.axis_index("dp"), lax.axis_index("gx"), lax.axis_index("yz"))
    sources = (v_hbm, k1_hbm, k2_hbm, b1_hbm, b2_hbm, up_hbm)
    targets = (v_ref, k1_ref, k2_ref, b1_ref, b2_ref, up_ref)
    loads = [
        pltpu.make_async_copy(source, target, load_sem.at[i])
        for i, (source, target) in enumerate(zip(sources, targets))
    ]
    for load in loads:
        load.start()
    plane = n_dp * n_yz
    rank = dp * n_yz + yz

    def plane_peer(k):
        other = lax.rem(rank + k, plane)
        return other, (other // n_yz, gx, lax.rem(other, n_yz))

    def gx_peer(k):
        other = lax.rem(gx + k, n_gx)
        return other, (dp, other, yz)

    def exists(dx, dz):
        inside = [gx + dx >= 0, gx + dx < n_gx, yz + dz >= 0, yz + dz < n_yz]
        return functools.reduce(jnp.logical_and, inside)

    barrier = pltpu.get_barrier_semaphore()
    for k in range(1, plane):
        pl.semaphore_signal(barrier, inc=1, device_id=plane_peer(k)[1], device_id_type=MESH)
    for k in range(1, n_gx):
        pl.semaphore_signal(barrier, inc=1, device_id=gx_peer(k)[1], device_id_type=MESH)
    corners = jnp.int32(0)
    for dx, dz in SIDES:
        if dx and dz:
            corners = corners + exists(dx, dz).astype(jnp.int32)

            @pl.when(exists(dx, dz))
            def _(dx=dx, dz=dz):
                pl.semaphore_signal(
                    barrier, inc=1, device_id=(dp, gx + dx, yz + dz), device_id_type=MESH
                )

    def piece(own, dx, dz):
        n = own.shape[0]
        i, j = (n - 1 if dx > 0 else 0, n - 1 if dz > 0 else 0)
        if dx and dz:
            return own.at[i, j]
        return own.at[i] if dx else own.at[:, j]

    def slot(bufs, dx, dz):
        i, j = (int(dx > 0), int(dz > 0))
        if dx and dz:
            return bufs[2].at[i, j]
        return bufs[0].at[i] if dx else bufs[1].at[j]

    sets = ((vol_x, vol_z, vol_d), (mid_x, mid_z, mid_d), (grad_x, grad_z, grad_d))
    for dx, dz in SIDES:

        @pl.when(jnp.logical_not(exists(dx, dz)))
        def _(dx=dx, dz=dz):
            for bufs in sets:
                missing = slot(bufs, dx, dz)
                missing[...] = jnp.zeros_like(missing)

    def halo_copy(turn, own, bufs, dx, dz):
        return pltpu.make_async_remote_copy(
            src_ref=piece(own, dx, dz),
            dst_ref=slot(bufs, -dx, -dz),
            send_sem=halo_send.at[turn, SIDES.index((dx, dz))],
            recv_sem=halo_recv.at[turn, SIDES.index((-dx, -dz))],
            device_id=(dp, gx + dx, yz + dz),
            device_id_type=MESH,
        )

    def halo_start(turn, own, bufs):
        for dx, dz in SIDES:

            @pl.when(exists(dx, dz))
            def _(dx=dx, dz=dz):
                halo_copy(turn, own, bufs, dx, dz).start()

    def halo_wait(turn, own, bufs):
        for dx, dz in SIDES:

            @pl.when(exists(dx, dz))
            def _(dx=dx, dz=dz):
                halo_copy(turn, own, bufs, dx, dz).wait_send()
                halo_copy(turn, own, bufs, -dx, -dz).wait_recv()

    lanes = lax.broadcasted_iota(jnp.int32, (1, 128), 1)
    cell_z = lanes % 32

    def raw(own, bufs, x, z, more):
        n = own.shape[0]
        dx = -1 if x < 0 else int(x >= n)
        dz = -1 if z < 0 else int(z >= n)
        if not dx and not dz:
            tile = own[(x, z) + more]
        elif dx and dz:
            tile = bufs[2][(int(dx > 0), int(dz > 0)) + more]
        elif dx:
            tile = bufs[0][(int(dx > 0), z) + more]
        else:
            tile = bufs[1][(int(dz > 0), x) + more]
        return tile

    def roll(tile, by):
        return pltpu.roll(tile, by % 128, 1)

    def along_z(own, bufs, x, z, more=()):
        n = own.shape[0]
        if 0 <= z < n:
            return raw(own, bufs, x, z, more)
        near = raw(own, bufs, x, n - 1 if z < 0 else 0, more).astype(F32)
        far = raw(own, bufs, x, z, more).astype(F32)
        if z < 0:
            return jnp.where(cell_z == 0, roll(far, -31), roll(near, 1))
        return jnp.where(cell_z == 31, roll(far, 31), roll(near, -1))

    def y_before(tile):
        return jnp.where(lanes < 32, 0.0, roll(tile, 32))

    def y_after(tile):
        return jnp.where(lanes >= 96, 0.0, roll(tile, -32))

    def places(first, end, inner):
        return [
            (x, z)
            for x in range(first, end)
            for z in range(first, end)
            if inner == (first < x < end - 1 and first < z < end - 1)
        ]

    def fill(target, own, bufs, flip, inner):
        rows = own.shape[3]
        for x, z in places(-1, 3, inner):
            ax, az = (x + 1, z + 1)
            tiles = [along_z(own, bufs, x, z, (y,)) for y in (0, 1)]
            after = y_after(tiles[0].astype(F32))
            before = y_before(tiles[1].astype(F32))
            for ay, tile in enumerate((before, tiles[0], tiles[1], after)):
                tile = tile.astype(BF16)
                for p, (px, pz, py) in enumerate(PHASES):
                    tap = (ax - px, ay - py, az - pz)
                    if tap in TAPS:
                        t = TAPS.index(tap)
                        t = 26 - t if flip else t
                        target[t * rows : (t + 1) * rows, p * 128 : (p + 1) * 128] = tile

    rows16 = lax.broadcasted_iota(jnp.int32, (16, 1), 0)

    def fill_patch(inner):
        for ex, ez in places(-1, 5, inner):
            tile = along_z(vol, sets[0], ex, ez).astype(F32)
            low = pltpu.roll(tile, 4, 0)
            low = jnp.where(rows16 < 4, y_before(low), low).astype(BF16)
            high = pltpu.roll(tile, 12, 0)
            high = jnp.where(rows16 >= 12, y_after(high), high).astype(BF16)
            for q, (qx, qz, qy) in enumerate(PHASES):
                ax, az = (ex + 1 - 2 * qx, ez + 1 - 2 * qz)
                if 0 <= ax < 4 and 0 <= az < 4:
                    row = ax * 64 + az * 16
                    patch[row : row + 16, q * 128 : (q + 1) * 128] = high if qy else low

    split[...] = one_hot(split_source(), 512)
    loads[0].wait()
    for c in range(4):
        values = v_ref[c].astype(F32)
        for y in range(16):
            fy, ry = (y // 4, y % 4)
            row = ry * 16 + c * 4
            cells[row : row + 4, fy * 128 : (fy + 1) * 128] = values[:, y * 128 : (y + 1) * 128]
    by_phase = dot(cells[...].astype(BF16), split[...]).astype(BF16)
    at = indices(64, 1)
    order = one_hot(at % 4 * 16 + at // 4, 64)
    by_phase = dot(order, by_phase).astype(BF16)
    for x in range(4):
        for rz in range(4):
            vol[x, rz] = by_phase[x * 16 : x * 16 + 16, rz * 128 : rz * 128 + 128]
    pl.semaphore_wait(barrier, plane + n_gx - 2 + corners)
    vol_bufs = sets[0]
    halo_start(0, vol, vol_bufs)

    fill_patch(True)
    for load in loads[1:]:
        load.wait()
    k1[...] = jnp.zeros_like(k1)
    for t in range(27):
        k1[t * 4 : t * 4 + 4, 0:32] = k1_ref[t].astype(F32)
    taps[...] = one_hot(tap_source(1), 128)
    flat_k1 = k1[...].T[0:32].astype(BF16)
    for p in range(8):
        chosen = dot(flat_k1, taps[:, p * 256 : (p + 1) * 256])
        w1[p * 32 : (p + 1) * 32, :] = chosen.astype(BF16)
    bias1 = jnp.broadcast_to(b1_ref[...], (128, 32)).T
    bias2 = jnp.broadcast_to(b2_ref[...], (128, 64)).T
    for j in range(7):
        rows = k2_ref[j * 128 : min(j * 128 + 128, 864), :].astype(F32)
        if j == 6:
            rows = jnp.concatenate([rows, jnp.zeros((32, 64), F32)], axis=0)
        k2f[:, j * 128 : (j + 1) * 128] = rows.T.astype(BF16)
    halo_wait(0, vol, vol_bufs)

    fill_patch(False)
    for qx in range(2):
        for qz in range(2):
            q = qx * 4 + qz * 2
            pre = dot(w1[...], patch[:, q * 128 : (q + 2) * 128])
            total = jnp.zeros((32, 256), F32)
            for p in range(8):
                value = pre[p * 32 : (p + 1) * 32] + jnp.concatenate([bias1, bias1], axis=1)
                pre1[p * 32 : (p + 1) * 32, q * 128 : (q + 2) * 128] = value
                total = total + leaky(value)
            for qy in range(2):
                own = total[:, qy * 128 : (qy + 1) * 128]
                mid[qx, qz, qy] = (own * 0.125).astype(BF16)

    mid_bufs = sets[1]
    halo_start(1, mid, mid_bufs)
    fill(im_mid, mid, mid_bufs, False, True)
    for t in range(0, 26, 2):
        pair = [k2_ref[u * 32 : (u + 1) * 32, :].astype(F32) for u in (t, t + 1)]
        k2b[:, t * 64 : (t + 2) * 64] = jnp.concatenate(pair, axis=1).astype(BF16)
    k2b[:, 1664:1728] = k2_ref[832:864, :]
    join[...] = one_hot(join_source(), 512)
    hot = lax.broadcasted_iota(jnp.int32, (2048, 128), 1) == tap_source(0)
    taps_t[...] = jnp.where(hot, 1.0, 0.0).astype(BF16)
    halo_wait(1, mid, mid_bufs)
    fill(im_mid, mid, mid_bufs, False, False)
    pre2 = dot(k2f[:, 0:864], im_mid[...])
    total = jnp.zeros((64, 128), F32)
    up = up_ref[...].astype(F32) * 0.125
    for p, (px, pz, py) in enumerate(PHASES):
        value = pre2[:, p * 128 : (p + 1) * 128] + bias2
        total = total + leaky(value)
        back = (up * slope_of(value)).astype(BF16)
        grad[px, pz, py] = back
        flat_grad[:, p * 128 : (p + 1) * 128] = back
    grad_bufs = sets[2]
    halo_start(2, grad, grad_bufs)
    feat_ref[...] = (total * 0.125).astype(BF16)

    two = dot_nt(flat_grad[...], im_mid[...])
    part_rows = 64 // plane
    part[:, :, 768:896] = jnp.zeros((plane, part_rows, 128), F32)
    part[:, :, 0:864] = two.reshape(plane, part_rows, 864)

    def rs_copy(k):
        other, device = plane_peer(k)
        return pltpu.make_async_remote_copy(
            src_ref=part.at[other], dst_ref=rs.at[k - 1],
            send_sem=plane_send.at[0, k - 1], recv_sem=plane_recv.at[0, k - 1],
            device_id=device, device_id_type=MESH,
        )

    def gx_copy(turn, buf, k):
        other, device = gx_peer(k)
        return pltpu.make_async_remote_copy(
            src_ref=buf.at[gx], dst_ref=buf.at[gx],
            send_sem=gx_send.at[turn, k - 1], recv_sem=gx_recv.at[turn, k - 1],
            device_id=device, device_id_type=MESH,
        )

    def plane_copy(turn, buf, k):
        other, device = plane_peer(k)
        return pltpu.make_async_remote_copy(
            src_ref=buf.at[rank], dst_ref=buf.at[rank],
            send_sem=plane_send.at[turn, k - 1], recv_sem=plane_recv.at[turn, k - 1],
            device_id=device, device_id_type=MESH,
        )

    for k in range(1, plane):
        rs_copy(k).start()

    fill(im_grad, grad, grad_bufs, True, True)
    halo_wait(2, grad, grad_bufs)
    fill(im_grad, grad, grad_bufs, True, False)
    rounded = dot(k2b[...], im_grad[...]).astype(BF16)

    for k in range(1, plane):
        rs_copy(k).wait()
    mine = part[rank]
    for k in range(1, plane):
        mine = mine + rs[k - 1]
    across[gx] = mine
    for k in range(1, n_gx):
        gx_copy(0, across, k).start()

    back1 = rounded.astype(F32) * 0.125
    for p in range(8):
        slope = slope_of(pre1[p * 32 : (p + 1) * 32, :])
        grads1[p * 32 : (p + 1) * 32, :] = (back1 * slope).astype(BF16)
    full = dot_nt(grads1[...], patch[...])
    full = jnp.concatenate([full[p * 32 : (p + 1) * 32] for p in range(8)], axis=1)
    high = full.astype(BF16)
    low = (full - high.astype(F32)).astype(BF16)
    folded = dot(jnp.concatenate([high, low], axis=0), taps_t[...])
    folded = folded[0:32] + folded[32:64]
    one_all[rank] = folded
    for k in range(1, plane):
        plane_copy(1, one_all, k).start()

    for px in range(2):
        joined = dot(rounded[:, px * 512 : (px + 1) * 512], join[...])
        pg_ref[:, px * 512 : (px + 1) * 512] = joined.astype(BF16)

    scale = 1.0 / n_dp
    for k in range(1, n_gx):
        gx_copy(0, across, k).wait()
    mine = across[0]
    for j in range(1, n_gx):
        mine = mine + across[j]
    gathered[rank] = mine * scale
    for k in range(1, plane):
        plane_copy(2, gathered, k).start()

    for k in range(1, plane):
        plane_copy(1, one_all, k).wait()
    mine = one_all[0]
    for j in range(1, plane):
        mine = mine + one_all[j]
    one_gx[gx] = mine
    for k in range(1, n_gx):
        gx_copy(1, one_gx, k).start()
    for k in range(1, plane):
        plane_copy(2, gathered, k).wait()
    whole = gathered[...].reshape(64, 896)
    for j in range(7):
        end = min(j * 128 + 128, 864)
        two_ref[j * 128 : end, :] = whole[:, j * 128 : (j + 1) * 128].T[0 : end - j * 128]
    for k in range(1, n_gx):
        gx_copy(1, one_gx, k).wait()
    mine = one_gx[0]
    for j in range(1, n_gx):
        mine = mine + one_gx[j]
    mine = (mine * scale).T
    for t in range(27):
        one_ref[t] = mine[t * 4 : t * 4 + 4]


def local(sizes, volume, kernel_one, bias_one, kernel_two, bias_two, upstream):
    n_dp, n_gx, n_yz = sizes
    plane = n_dp * n_yz
    rows = 64 // plane
    vmem = pl.BlockSpec(memory_space=pltpu.VMEM)

    def halos(n, more, rows):
        tile = more + (rows, 128)
        shapes = [(n, n), (2, n), (2, n), (2, 2)]
        return [pltpu.VMEM(s + tile, BF16) for s in shapes]

    feat, pg, one, two = pl.pallas_call(
        functools.partial(kernel, sizes),
        out_shape=(
            jax.ShapeDtypeStruct((64, 128), BF16),
            jax.ShapeDtypeStruct((32, 1024), BF16),
            jax.ShapeDtypeStruct((27, 4, 32), F32),
            jax.ShapeDtypeStruct((864, 64), F32),
        ),
        in_specs=[pl.BlockSpec(memory_space=pltpu.HBM)] * 6,
        out_specs=(vmem,) * 4,
        scratch_shapes=[
            *halos(4, (), 16),
            *halos(2, (2,), 32),
            *halos(2, (2,), 64),
            pltpu.VMEM((256, 256), BF16),
            pltpu.VMEM((256, 1024), BF16),
            pltpu.VMEM((256, 1024), F32),
            pltpu.VMEM((864, 1024), BF16),
            pltpu.VMEM((1728, 1024), BF16),
            pltpu.VMEM((64, 1024), BF16),
            pltpu.VMEM((plane, rows, 896), F32),
            pltpu.VMEM((plane - 1, rows, 896), F32),
            pltpu.VMEM((n_gx, rows, 896), F32),
            pltpu.VMEM((plane, rows, 896), F32),
            pltpu.VMEM((plane, 32, 128), F32),
            pltpu.VMEM((n_gx, 32, 128), F32),
            pltpu.VMEM((64, 512), F32),
            pltpu.VMEM((128, 128), F32),
            pltpu.VMEM((64, 896), BF16),
            pltpu.VMEM((32, 1728), BF16),
            pltpu.VMEM((512, 512), BF16),
            pltpu.VMEM((512, 512), BF16),
            pltpu.VMEM((128, 2048), BF16),
            pltpu.VMEM((2048, 128), BF16),
            pltpu.VMEM((256, 1024), BF16),
            pltpu.VMEM((4, 4, 2048), BF16),
            pltpu.VMEM((64, 128), BF16),
            pltpu.VMEM((27, 4, 32), BF16),
            pltpu.VMEM((1, 32), F32),
            pltpu.VMEM((864, 64), BF16),
            pltpu.VMEM((1, 64), F32),
            pltpu.SemaphoreType.DMA((6,)),
            pltpu.SemaphoreType.DMA((3, 8)),
            pltpu.SemaphoreType.DMA((3, 8)),
            pltpu.SemaphoreType.DMA((3, plane - 1)),
            pltpu.SemaphoreType.DMA((3, plane - 1)),
            pltpu.SemaphoreType.DMA((2, n_gx - 1)),
            pltpu.SemaphoreType.DMA((2, n_gx - 1)),
        ],
        compiler_params=pltpu.CompilerParams(
            collective_id=0, has_side_effects=True, vmem_limit_bytes=64 * 2**20 - 65536
        ),
        cost_estimate=pl.CostEstimate(
            flops=900_000_000, bytes_accessed=3_000_000, transcendentals=0
        ),
    )(
        volume.reshape(4, 4, 2048),
        upstream.reshape(64, 128),
        jnp.transpose(kernel_one, (2, 3, 4, 1, 0)).reshape(27, 4, 32),
        bias_one.reshape(1, 32),
        jnp.transpose(kernel_two, (2, 3, 4, 1, 0)).reshape(864, 64),
        bias_two.reshape(1, 64),
    )
    return (
        feat.reshape(1, 64, 1, 1, 128),
        pg.reshape(1, 32, 2, 1, 512),
        jnp.transpose(one.reshape(3, 3, 3, 4, 32), (4, 3, 0, 1, 2)),
        jnp.transpose(two.reshape(3, 3, 3, 32, 64), (4, 3, 0, 1, 2)),
    )


def wide_with_halo(shard, sides, width):
    for axis, dim in sides:
        size, length = (lax.axis_size(axis), shard.shape[dim])
        up = [(i, (i + 1) % size) for i in range(size - 1)]
        down = [(j, i) for i, j in up]
        last = lax.slice_in_dim(shard, length - width, length, axis=dim)
        leading = lax.slice_in_dim(shard, 0, width, axis=dim)
        before = lax.ppermute(last, axis, up)
        after = lax.ppermute(leading, axis, down)
        shard = jnp.concatenate([before, shard, after], axis=dim)
    return shard


def wide_passed_along(value, axis, steps):
    count = lax.axis_size(axis)
    leading, last = (max(0, -steps), min(count, count - steps))
    return lax.ppermute(value, axis, [(source, source + steps) for source in range(leading, last)])


def wide_correlate(padded, kernel):
    return lax.conv_general_dilated(
        padded,
        kernel,
        (1, 1, 1),
        "VALID",
        dimension_numbers=("NCDHW", "OIDHW", "NCDHW"),
        preferred_element_type=jnp.float32,
    )


def wide_kernel_grad(padded, grads):
    summed = lax.conv_general_dilated(
        padded,
        grads,
        (1, 1, 1),
        "VALID",
        dimension_numbers=("CNDHW", "IODHW", "NCDHW"),
        preferred_element_type=jnp.float32,
    )
    return jnp.transpose(summed, (1, 0, 2, 3, 4))


def wide_average_pool(field):
    extent = field.shape
    shaped = field.reshape(
        extent[0], extent[1], extent[2] // 2, 2, extent[3] // 2, 2, extent[4] // 2, 2
    )
    return jnp.mean(shaped, axis=(3, 5, 7))


def wide_spread_back(field):
    extent = field.shape
    wide = jnp.broadcast_to(
        field[:, :, :, None, :, None, :, None],
        (extent[0], extent[1], extent[2], 2, extent[3], 2, extent[4], 2),
    )
    return wide.reshape(extent[0], extent[1], extent[2] * 2, extent[3] * 2, extent[4] * 2)


def wide_leaky(values):
    return jnp.where(values > 0, values, SLOPE * values)


def wide_slope_of(values):
    return jnp.where(values > 0, 1.0, SLOPE).astype(values.dtype)


def wide_unfold(blocks, block_y, block_z):
    extent = blocks.shape
    return blocks[:, :, :, 0].reshape(extent[0], extent[1], extent[2], block_y, block_z)


def wide_refold(field):
    extent = field.shape
    return field.reshape(extent[0], extent[1], extent[2], 1, extent[3] * extent[4])


def wide_extend(field):
    z_index = lax.axis_index("yz") % ZPARTS
    extended = wide_with_halo(field, (("gx", 2),), 1)
    incoming = []
    for offset, boundary in ((ZPARTS, extended[:, :, :, -1:]), (-ZPARTS, extended[:, :, :, :1])):
        incoming.append(wide_passed_along(boundary, "yz", offset))
    extended = jnp.concatenate([incoming[0], extended, incoming[1]], axis=3)
    arrived = []
    for offset, boundary, keeper in (
        (1, extended[:, :, :, :, -1:], z_index > 0),
        (-1, extended[:, :, :, :, :1], z_index < ZPARTS - 1),
    ):
        moved = wide_passed_along(boundary, "yz", offset)
        arrived.append(jnp.where(keeper, moved, jnp.zeros_like(moved)))
    return jnp.concatenate([arrived[0], extended, arrived[1]], axis=4)


def wide_local(volume, kernel_one, bias_one, kernel_two, bias_two, upstream):
    field = wide_unfold(volume, BY, BZ)
    padded_in = wide_extend(field)
    first_pre = wide_correlate(padded_in, kernel_one) + bias_one[None, :, None, None, None]
    pooled_one = wide_average_pool(wide_leaky(first_pre)).astype(jnp.bfloat16)
    padded_mid = wide_extend(pooled_one)
    second_pre = wide_correlate(padded_mid, kernel_two) + bias_two[None, :, None, None, None]
    features = wide_average_pool(wide_leaky(second_pre)).astype(jnp.bfloat16)
    cotangent = wide_unfold(upstream, BY // 4, BZ // 4).astype(jnp.float32)
    second_grad = (wide_spread_back(cotangent) * 0.125 * wide_slope_of(second_pre)).astype(jnp.bfloat16)
    two_grad = wide_kernel_grad(padded_mid, second_grad)
    replicas = lax.axis_size("dp") * volume.shape[0]
    padded_grad = wide_extend(second_grad)
    flipped = jnp.transpose(jnp.flip(kernel_two, (2, 3, 4)), (1, 0, 2, 3, 4))
    pooled_grad = wide_correlate(padded_grad, flipped).astype(jnp.bfloat16)
    first_grad = (
        wide_spread_back(pooled_grad.astype(jnp.float32)) * 0.125 * wide_slope_of(first_pre)
    ).astype(jnp.bfloat16)
    one_grad = wide_kernel_grad(padded_in, first_grad)
    one_grad, two_grad = lax.psum((one_grad, two_grad), ("dp", "gx", "yz"))
    return (wide_refold(features), wide_refold(pooled_grad), one_grad / replicas, two_grad / replicas)


def solution(mesh):
    sizes = tuple(mesh.shape[name] for name in ("dp", "gx", "yz"))
    one_row = sizes[2] == ZPARTS and 64 % (8 * sizes[0] * sizes[2]) == 0
    return jax.shard_map(
        functools.partial(local, sizes) if one_row else wide_local,
        mesh=mesh,
        in_specs=(
            P("dp", None, "gx", "yz", None),
            P(),
            P(),
            P(),
            P(),
            P("dp", None, "gx", "yz", None),
        ),
        out_specs=(P("dp", None, "gx", "yz", None), P("dp", None, "gx", "yz", None), P(), P()),
        check_vma=False,
    )
```
